32 devices in a mesh: rad: 4 (over x, core), lat: 8 (over z, y).
Axes of the slice: x: 2, y: 2, z: 4, core: 2. Of those that a mesh axis runs over, the one named last changes fastest.
Arguments:
- velocity: bfloat16 [3, 128, 768, 1536], P(None, 'rad', 'lat'), may hold values from -6 to 6
- density: float32 [128], P('rad'), may hold values from 0.3 to 3
- offsets: int32 [4], replicated, may hold values from -3 to 3, as said below
- radial_weights: float32 [2, 4, 128], P(None, None, 'rad'), may hold values from -3 to 3
- angular_scale: float32 [128], P('rad'), may hold values from 9.536743e-07 to 3.8146973e-06
- order_table: int32 [512], replicated, may hold values from 0 to 511, as said below
- eigenfunctions: float32 [512, 32, 128], P(None, None, 'rad'), may hold values from -0.5 to 0.5
Outputs:
- coeffs: float32 [512, 2, 32, 512], P('lat', None, 'rad')
The draws below stay inside these ranges and needn't reach their ends.
Inputs may be any that keep to these rules, and one draw needn't show every extreme that they name: 4 distinct offsets; minus 3 and 3 are among them. `order_table`: a permutation of the orders; for every k, slots 2k and 2k + 1 hold orders m and 511 - m.
All inputs are finite; a program needn't handle non-finite values.
Results may differ from the reference program's by a relative error of at most 0.0003.
Values sent between devices are 32-bit elements; how exact they have to be, the bound alone decides.
A program may use at most 256 MiB of HBM per device.

```python
import math
import jax
import jax.numpy as jnp
from jax import lax

NLON = 1536
NLAT = 768
LDEG = 512
NMODE = 32
TAPS = 4
HALO = 3
NR = 128


def draw_offsets(key, part):
    first, second = jax.random.split(jax.random.fold_in(key, 11))
    inner = jax.random.permutation(first, 2 * HALO - 1)[:TAPS - 2].astype(jnp.int32) - (HALO - 1)
    taps = jnp.concatenate([jnp.array([-HALO, HALO], jnp.int32), inner])
    return jax.random.permutation(second, taps)


def draw_order_table(key, part):
    first, second = jax.random.split(jax.random.fold_in(key, 23))
    pairs = jax.random.permutation(first, LDEG // 2).astype(jnp.int32)
    flips = jax.random.randint(second, (LDEG // 2,), 0, 2, dtype=jnp.int32)
    lower = jnp.where(flips == 1, LDEG - 1 - pairs, pairs)
    upper = LDEG - 1 - lower
    return jnp.stack([lower, upper], axis=1).reshape(LDEG)


def block_scale(stream_key, extent, shards, least, top_value):
    def one(position, parts):
        draws = jax.random.uniform(jax.random.fold_in(jax.random.fold_in(stream_key, 6), position), (parts,), jnp.float32, least / len(shards), top_value / len(shards))
        return jnp.repeat(jnp.exp(draws), extent[position] // parts).reshape((-1,) + (1,) * (len(extent) - position - 1))

    loudness = one(*shards[0])
    for cut in shards[1:]:
        loudness = loudness * one(*cut)
    return loudness


def scatter_about(own_key, shape, deviation, most, shards=(), kind=jnp.bfloat16):
    values = deviation * jax.random.normal(own_key, shape, jnp.float32)
    if shards:
        values = values * block_scale(own_key, shape, shards, -0.22, 0.18)
    return jnp.clip(values, -most, most).astype(kind)


def setup_inputs(seed: int = 0) -> dict:
    splits = jax.random.split(jax.random.key(seed), 8)
    velocity = scatter_about(splits[0], (3, NR, NLAT, NLON), 1.0, 6.0, ((1, 4), (2, 8)))
    density = jnp.clip(jnp.exp(math.log(3.0) - 2.3025851 * jax.random.uniform(splits[1], (NR,), jnp.float32) ** block_scale(splits[1], (NR,), ((0, 4),), -0.2, 0.2)), 0.3, 3.0)
    offsets = draw_offsets(jax.random.fold_in(splits[7], 71), 0)
    radial_weights = scatter_about(splits[3], (2, TAPS, NR), 0.5, 3.0, ((2, 4),), jnp.float32)
    angular_scale = jnp.clip(jnp.exp(math.log(3.814697265625e-06) - 1.3862944 * jax.random.uniform(splits[4], (NR,), jnp.float32) ** block_scale(splits[4], (NR,), ((0, 4),), -0.2, 0.2)), 9.5367431640625e-07, 3.814697265625e-06)
    order_table = draw_order_table(jax.random.fold_in(splits[7], 71), 0)
    eigenfunctions = scatter_about(splits[6], (LDEG, NMODE, NR), NR ** -0.5, 0.5, ((2, 4),), jnp.float32)
    return dict(velocity=velocity, density=density, offsets=offsets, radial_weights=radial_weights, angular_scale=angular_scale, order_table=order_table, eigenfunctions=eigenfunctions)


def legendre_rows(orders, lat_count, degrees):
    colatitude = jnp.pi * (jnp.arange(lat_count, dtype=jnp.float32) + 0.5) / lat_count
    cosine = jnp.cos(colatitude)
    sine = jnp.sin(colatitude)
    order_float = orders.astype(jnp.float32)
    ladder = jnp.arange(1, degrees, dtype=jnp.float32)
    log_steps = jnp.concatenate([jnp.zeros((1,), jnp.float32), jnp.cumsum(0.5 * jnp.log((2.0 * ladder + 1.0) / (2.0 * ladder)))])
    log_start = 0.5 * jnp.log(jnp.ones((), jnp.float32) * 0.5) + jnp.take(log_steps, orders)
    log_diagonal = log_start[:, None] + order_float[:, None] * jnp.log(sine)[None, :]

    def advance(state, degree):
        previous, older, exponent = state
        level = degree.astype(jnp.float32)
        upward = jnp.sqrt((4.0 * level * level - 1.0) / jnp.maximum(level * level - order_float * order_float, 1.0))
        backward = jnp.sqrt(jnp.maximum((level - 1.0) * (level - 1.0) - order_float * order_float, 0.0) / jnp.maximum(4.0 * (level - 1.0) * (level - 1.0) - 1.0, 1.0))
        recurred = upward[:, None] * (cosine[None, :] * previous - backward[:, None] * older)
        starting = (degree == orders)[:, None]
        scaled = jnp.where(starting, jnp.ones_like(recurred), jnp.where((degree > orders)[:, None], recurred, jnp.zeros_like(recurred)))
        exponent = jnp.where(starting, log_diagonal, exponent)
        ratio = jnp.maximum(jnp.abs(scaled), 1.0)
        scaled = scaled / ratio
        previous = previous / ratio
        exponent = exponent + jnp.log(ratio)
        return ((scaled, previous, exponent), (scaled, exponent))
    zeros = jnp.zeros((orders.shape[0], lat_count), jnp.float32)
    _, outputs = lax.scan(advance, (zeros, zeros, zeros), jnp.arange(degrees, dtype=jnp.int32), unroll=32)
    rows = outputs[0] * jnp.exp(outputs[1])
    weight = jnp.sqrt(jnp.pi / lat_count) * sine
    return rows * weight[None, None, :]

def spectral_source(part, rows):
    transformed = jnp.einsum('fijco,loj->fiocl', part, rows, precision=lax.Precision.HIGHEST)
    level = jnp.arange(rows.shape[0], dtype=jnp.float32)
    degree_factor = level * (level + 1.0)
    return transformed[0] - degree_factor * transformed[1]

def grid_fields(flow, density, padded, offsets, radial_weights, angular_scale):
    radial, polar, azimuth = (flow[0], flow[1], flow[2])
    rho = density[:, None, None]
    shells = flow.shape[1]
    radial_term = jnp.zeros_like(radial)
    for tap in range(TAPS):
        shifted = lax.dynamic_slice_in_dim(padded, (HALO + offsets[tap]).astype(jnp.int32), shells, 1)
        radial_term = radial_term + radial_weights[0, tap][:, None, None] * shifted[0] + radial_weights[1, tap][:, None, None] * shifted[1]
    angular_term = angular_scale[:, None, None] * rho * (polar * polar + azimuth * azimuth - 2.0 * radial * radial + polar * azimuth)
    return (radial_term, angular_term)

def reference(velocity, density, offsets, radial_weights, angular_scale, order_table, eigenfunctions):
    lat_block = math.gcd(NLAT, 16)
    lat_blocks = NLAT // lat_block

    def band(block):
        flow = lax.dynamic_slice_in_dim(velocity, block * lat_block, lat_block, 2).astype(jnp.float32)
        rho = density[:, None, None]
        cross = jnp.stack([rho * flow[0] * flow[1], rho * flow[0] * flow[2]])
        padded = jnp.pad(cross, ((0, 0), (HALO, HALO), (0, 0), (0, 0)))
        radial_term, angular_term = grid_fields(flow, density, padded, offsets, radial_weights, angular_scale)
        fields = jnp.stack([radial_term, angular_term])
        waves = jnp.fft.rfft(fields, axis=-1)[..., :LDEG] / jnp.sqrt(jnp.ones((), jnp.float32) * NLON)
        return jnp.stack([jnp.real(waves), jnp.imag(waves)], axis=3)
    bands = lax.map(band, jnp.arange(lat_blocks, dtype=jnp.int32))
    spectrum = jnp.moveaxis(bands, 0, 2).reshape(2, NR, NLAT, 2, LDEG)
    order_block = 16

    def order_group(block):
        orders = (block * order_block + jnp.arange(order_block, dtype=jnp.int32)).astype(jnp.int32)
        rows = legendre_rows(orders, NLAT, LDEG)
        part = lax.dynamic_slice_in_dim(spectrum, block * order_block, order_block, 4)
        source = spectral_source(part, rows)
        return jnp.einsum('rocl,lnr->ocnl', source, eigenfunctions, precision=lax.Precision.HIGHEST)
    natural = lax.map(order_group, jnp.arange(LDEG // order_block, dtype=jnp.int32))
    natural = natural.reshape(LDEG, 2, NMODE, LDEG)
    return jnp.take(natural, order_table, axis=0)
```

```python
import math

import jax
import jax.numpy as jnp
from jax import lax
from jax.experimental import pallas as pl
from jax.experimental.pallas import tpu as pltpu
from jax.sharding import PartitionSpec as P

TAPS = 4
HALO = 3
STEP = 8
LANES = 128
SHIFT = 60
CHUNKS = 4
HIGH = lax.Precision.HIGH


def extended(value, sides, width):
    for axis, dim in sides:
        size, length = (lax.axis_size(axis), value.shape[dim])
        up = [(i, (i + 1) % size) for i in range(size - 1)]
        down = [(j, i) for i, j in up]
        last = lax.slice_in_dim(value, length - width, length, axis=dim)
        initial = lax.slice_in_dim(value, 0, width, axis=dim)
        before = lax.ppermute(last, axis, up)
        after = lax.ppermute(initial, axis, down)
        value = jnp.concatenate([before, value, after], axis=dim)
    return value


def ladder_kernel(up_ref, down_ref, cosine_ref, first_ref, power_ref, order_ref, weight_ref, out_ref,
                  now, older, power):
    block = pl.program_id(0)

    @pl.when(block == 0)
    def _():
        now[...] = jnp.zeros_like(now)
        older[...] = jnp.zeros_like(older)
        power[...] = power_ref[...]

    current, previous, scale = now[...], older[...], power[...]
    factor = jnp.where(
        scale == 0.0,
        1.0,
        jnp.where(
            scale == -1.0, 2.0**-SHIFT, jnp.where(scale == -2.0, 2.0 ** (-2 * SHIFT), 0.0)
        ),
    )
    factor = factor * weight_ref[...]
    cosine = cosine_ref[...]
    first = first_ref[...]
    orders = order_ref[...]
    for i in range(STEP):
        recurred = up_ref[0, :, i : i + 1] * (cosine * current) - down_ref[0, :, i : i + 1] * previous
        begins = orders == block * STEP + i
        recurred = recurred + jnp.where(begins, first, 0.0)
        previous = current
        current = recurred
        out_ref[i] = recurred * factor
    large = jnp.maximum(jnp.abs(current), jnp.abs(previous)) > 2.0**SHIFT
    shrink = jnp.where(large, 2.0**-SHIFT, 1.0)
    now[...] = current * shrink
    older[...] = previous * shrink
    power[...] = scale + jnp.where(large, 1.0, 0.0)


def legendre_rows(orders, first_lat, lat_local, lat_count, degrees):
    count = orders.shape[0]
    padded = -(-lat_local // LANES) * LANES
    lat = first_lat + jnp.minimum(jnp.arange(padded, dtype=jnp.int32), lat_local - 1)
    colatitude = jnp.pi * (lat.astype(jnp.float32) + 0.5) / lat_count
    cosine = jnp.cos(colatitude)
    sine = jnp.sin(colatitude)
    order_float = orders.astype(jnp.float32)
    ladder = jnp.arange(1, degrees, dtype=jnp.float32)
    log_steps = jnp.concatenate(
        [
            jnp.zeros((1,), jnp.float32),
            jnp.cumsum(0.5 * jnp.log((2.0 * ladder + 1.0) / (2.0 * ladder))),
        ]
    )
    log_start = 0.5 * jnp.log(jnp.ones((), jnp.float32) * 0.5) + jnp.take(log_steps, orders)
    log_diagonal = log_start[:, None] + order_float[:, None] * jnp.log(sine)[None, :]
    unit = SHIFT * 0.6931471805599453
    power = jnp.minimum(jnp.floor(log_diagonal / unit), 0.0)
    coarse = 41.5
    first = jnp.exp((log_diagonal - power * coarse) - power * (unit - coarse))
    level = jnp.arange(degrees, dtype=jnp.float32)[None, :]
    square = (order_float * order_float)[:, None]
    upward = jnp.sqrt((4.0 * level * level - 1.0).clip(0.0) / jnp.maximum(level * level - square, 1.0))
    below = (level - 1.0) * (level - 1.0)
    backward = jnp.sqrt(
        jnp.maximum(below - square, 0.0) / jnp.maximum(4.0 * below - 1.0, 1.0)
    )

    def stepped(value):
        return value.reshape(count, degrees // STEP, STEP).transpose(1, 0, 2)

    weight = jnp.where(
        jnp.arange(padded) < lat_local, jnp.sqrt(jnp.pi / lat_count) * sine, 0.0
    )
    whole = pl.BlockSpec((count, padded), lambda k: (0, 0))
    row = pl.BlockSpec((1, padded), lambda k: (0, 0))
    coefficient = pl.BlockSpec((1, count, STEP), lambda k: (k, 0, 0))
    return pl.pallas_call(
        ladder_kernel,
        grid=(degrees // STEP,),
        in_specs=[coefficient, coefficient, row, whole, whole, whole, row],
        out_specs=pl.BlockSpec((STEP, count, padded), lambda k: (k, 0, 0)),
        out_shape=jax.ShapeDtypeStruct((degrees, count, padded), jnp.float32),
        scratch_shapes=[pltpu.VMEM((count, padded), jnp.float32)] * 3,
        compiler_params=pltpu.CompilerParams(vmem_limit_bytes=16 << 20),
        cost_estimate=pl.CostEstimate(
            flops=20 * degrees * count * padded,
            bytes_accessed=4 * degrees * count * padded,
            transcendentals=0,
        ),
    )(
        stepped(upward),
        stepped(upward * backward),
        cosine[None, :],
        first,
        power,
        jnp.broadcast_to(orders[:, None], (count, padded)),
        weight[None, :],
    )


def split(value):
    high = value.astype(jnp.bfloat16)
    return high, (value - high.astype(jnp.float32)).astype(jnp.bfloat16)


def degree_kernel(rows_ref, part_ref, out_ref):
    degrees = rows_ref.shape[0]
    half = part_ref.shape[1] // 2
    shells = out_ref.shape[3]
    level = lax.broadcasted_iota(jnp.int32, (degrees, half), 0).astype(jnp.float32)
    factor = level * (level + 1.0)
    contract = (((1,), (1,)), ((), ()))
    for o in range(part_ref.shape[0]):
        rows_high, rows_low = split(rows_ref[:, o, :])
        high, low = split(part_ref[o])
        both = jnp.concatenate([rows_high, rows_low], axis=1)
        twice = jnp.concatenate([high, high], axis=1)
        sums = lax.dot_general(both, twice, contract, preferred_element_type=jnp.float32)
        sums = sums + lax.dot_general(rows_high, low, contract, preferred_element_type=jnp.float32)
        source = sums[:, :half] - factor * sums[:, half:]
        for c in range(2):
            out_ref[c, :, o, :] = source[:, c * shells : (c + 1) * shells]


def spectral_source(part, rows, first, count):
    degrees, _, padded = rows.shape
    columns = part.shape[1]
    shells = columns // 4
    group = 8
    skip = first // group
    return pl.pallas_call(
        degree_kernel,
        grid=(count // group,),
        in_specs=[
            pl.BlockSpec((degrees, group, padded), lambda k: (0, skip + k, 0)),
            pl.BlockSpec((group, columns, padded), lambda k: (k, 0, 0)),
        ],
        out_specs=pl.BlockSpec((2, degrees, group, shells), lambda k: (0, 0, k, 0)),
        out_shape=jax.ShapeDtypeStruct((2, degrees, count, shells), jnp.float32),
        compiler_params=pltpu.CompilerParams(vmem_limit_bytes=48 << 20),
        cost_estimate=pl.CostEstimate(
            flops=6 * degrees * count * columns * padded,
            bytes_accessed=4 * count * (degrees * padded + columns * padded + degrees * 2 * shells),
            transcendentals=0,
        ),
    )(rows, part)


def fourier_table(lon_count, orders):
    longitude = jnp.arange(lon_count, dtype=jnp.int32)[None, :, None]
    angle = (
        2.0
        * jnp.pi
        * (longitude * orders[:, None, :] % lon_count).astype(jnp.float32)
        / lon_count
    )
    scale = 1.0 / jnp.sqrt(jnp.ones((), jnp.float32) * lon_count)
    return jnp.concatenate([jnp.cos(angle), -jnp.sin(angle)], axis=2) * scale


def body(velocity, density, offsets, radial_weights, angular_scale, order_table, eigenfunctions):
    shells = velocity.shape[1]
    lat_local = velocity.shape[2]
    lon_count = velocity.shape[3]
    degrees = order_table.shape[0]
    lat_groups = lax.axis_size("lat")
    rad_groups = lax.axis_size("rad")
    per_device = degrees // lat_groups
    lat_count = lat_local * lat_groups
    flow = velocity.astype(jnp.float32)
    radial, polar, azimuth = (flow[0], flow[1], flow[2])
    rho = density[:, None, None]
    cross = jnp.stack([rho * radial * polar, rho * radial * azimuth])
    padded = extended(cross, (("rad", 1),), HALO)
    radial_term = jnp.zeros_like(radial)
    for tap in range(TAPS):
        shifted = lax.dynamic_slice_in_dim(padded, HALO + offsets[tap], shells, 1)
        radial_term = (
            radial_term
            + radial_weights[0, tap][:, None, None] * shifted[0]
            + radial_weights[1, tap][:, None, None] * shifted[1]
        )
    angular_term = (
        angular_scale[:, None, None]
        * rho
        * (polar * polar + azimuth * azimuth - 2.0 * radial * radial + polar * azimuth)
    )
    fields = jnp.stack([radial_term, angular_term]).reshape(2 * shells * lat_local, lon_count)
    quarter = per_device // rad_groups
    count = degrees // rad_groups
    chunks = math.gcd(CHUNKS, quarter)
    size = count // chunks
    slot_order = (
        order_table.reshape(lat_groups, rad_groups, chunks, quarter // chunks)
        .transpose(1, 2, 0, 3)
        .reshape(rad_groups, chunks, size)
    )
    received = []
    for chunk in range(chunks):
        spectrum = jnp.einsum(
            "dkx,nk->dxn",
            fourier_table(lon_count, slot_order[:, chunk]),
            fields,
            precision=HIGH,
            preferred_element_type=jnp.float32,
        )
        received.append(
            lax.all_to_all(spectrum, "rad", split_axis=0, concat_axis=0, tiled=True)
        )
    my_orders = lax.dynamic_index_in_dim(
        slot_order, lax.axis_index("rad"), 0, keepdims=False
    ).reshape(count)
    rows = legendre_rows(
        my_orders, lax.axis_index("lat") * lat_local, lat_local, lat_count, degrees
    )
    modes = lax.all_gather(eigenfunctions, "rad", axis=2, tiled=True)
    mine = []
    for chunk in range(chunks):
        part = received[chunk].reshape(rad_groups, 2, size, 2, shells, lat_local)
        part = jnp.pad(part, ((0, 0),) * 5 + ((0, rows.shape[2] - lat_local),))
        part = part.transpose(2, 3, 1, 0, 4, 5).reshape(size, 4 * rad_groups * shells, -1)
        source = spectral_source(part, rows, chunk * size, size)
        totals = jnp.einsum("clor,lnr->ocnl", source, modes, precision=HIGH)
        mine.append(lax.psum_scatter(totals, "lat", scatter_dimension=0, tiled=True))
    mine = jnp.concatenate(mine, axis=0)
    return lax.all_to_all(mine, "rad", split_axis=2, concat_axis=0, tiled=True)


def solution(mesh):
    placed = (
        P(None, "rad", "lat", None),
        P("rad"),
        P(),
        P(None, None, "rad"),
        P("rad"),
        P(),
        P(None, None, "rad"),
    )
    return jax.shard_map(
        body, mesh=mesh, in_specs=placed, out_specs=P("lat", None, "rad", None), check_vma=False
    )
```
